256 devices in a mesh: row: 16 (over x, y_hi, core), col: 16 (over y_lo, z).
Axes of the slice: x: 4, y: 4 (y_hi: 2, y_lo: 2; y = y_hi * 2 + y_lo), z: 8, core: 2. Of those that a mesh axis runs over, the one named last changes fastest.
Arguments:
- iterate: float32 [96, 32, 128, 128], P('row', 'col'), may hold values from -1.2 to 1.2
- kept_cols: int32 [96, 32], P('row', 'col'), may hold values from 0 to 95, as said below
Outputs:
- square: float32 [96, 32, 128, 128], P('row', 'col')
- update: float32 [96, 32, 128, 128], P('row', 'col')
The draws below stay inside these ranges and needn't reach their ends.
Inputs may be any that keep to these rules, and one draw needn't show every extreme that they name: kept_cols[i, s] lies among block columns g * 96 // 16 to (g + 1) * 96 // 16 - 1 with g = s // 2; the entries of one row are distinct, and every row keeps its own diagonal block i.
All inputs are finite; a program needn't handle non-finite values.
Results may differ from the reference program's by a relative error of at most 0.0003.
Values sent between devices are 32-bit elements; how exact they have to be, the bound alone decides.
No kernel may reach another device: no remote copies, remote signals or barrier semaphores. Data moves between devices by JAX's collectives and lax.ppermute only.
A program may use at most 192 MiB of HBM per device.

```python
import jax
import jax.numpy as jnp
from jax import lax

BS = 128
SLOT = 2
NB = 96
KEEP = 32
N_COL = 16


def draw_kept_cols(key, part):
    key = jax.random.fold_in(key, 11)
    span_cols = NB // N_COL
    drawn = jax.random.randint(key, (NB, N_COL, span_cols), 0, 2 ** 20)
    offsets = jnp.arange(span_cols, dtype=jnp.int32)
    groups = jnp.arange(N_COL, dtype=jnp.int32)
    row_ids = jnp.arange(NB, dtype=jnp.int32)
    column_ids = groups[None, :, None] * span_cols + offsets[None, None, :]
    scores = jnp.where(column_ids == row_ids[:, None, None], -1, drawn * span_cols + offsets[None, None, :])
    ranking = jnp.argsort(scores, axis=-1, stable=True)[:, :, :SLOT].astype(jnp.int32)
    chosen = groups[None, :, None] * span_cols + ranking
    return chosen.reshape(NB, N_COL * SLOT).astype(jnp.int32)


def levels(own_key, shape, cuts, low, top_value):
    level = 1.0
    for position, shards_of in cuts:
        heights = jax.random.uniform(jax.random.fold_in(jax.random.fold_in(own_key, 6), position), (shards_of,), jnp.float32, low / len(cuts), top_value / len(cuts))
        level = level * jnp.repeat(jnp.exp(heights), shape[position] // shards_of).reshape((-1,) + (1,) * (len(shape) - 1 - position))
    return level


def centred(stream_key, shape, scale, limit, pieces=(), held_as=jnp.bfloat16):
    result = scale * jax.random.normal(stream_key, shape, jnp.float32)
    if pieces:
        result = result * levels(stream_key, shape, pieces, -0.22, 0.18)
    return jnp.clip(result, -limit, limit).astype(held_as)


def setup_inputs(seed: int = 0) -> dict:
    key_list = jax.random.split(jax.random.key(seed), 3)
    iterate = centred(key_list[0], (NB, KEEP, BS, BS), 0.2, 1.2, ((0, 16), (1, 16)), jnp.float32)
    kept_cols = draw_kept_cols(jax.random.fold_in(key_list[2], 71), 0)
    return dict(iterate=iterate, kept_cols=kept_cols)


def reference(iterate, kept_cols):
    def row_square(index):
        own_ids = kept_cols[index]
        own_vals = iterate[index]
        far_vals = jnp.take(iterate, own_ids, axis=0)
        far_ids = jnp.take(kept_cols, own_ids, axis=0)
        selected = jnp.zeros((KEEP, KEEP, BS, BS), jnp.float32)
        for offset in range(SLOT):
            columns = (jnp.arange(KEEP, dtype=jnp.int32) // SLOT) * SLOT + offset
            blocks = jnp.take(far_vals, columns, axis=1)
            matches = (jnp.take(far_ids, columns, axis=1) == own_ids[None, :]).astype(jnp.float32)
            selected = selected + matches[:, :, None, None] * blocks
        return jnp.einsum("tab,tsbc->sac", own_vals, selected, precision=lax.Precision.HIGHEST, preferred_element_type=jnp.float32)

    square = lax.map(row_square, jnp.arange(NB, dtype=jnp.int32))
    update = 1.5 * iterate - 0.5 * square
    return square, update
```

```python
import functools

import jax
import jax.numpy as jnp
import numpy as np
from jax import lax
from jax.experimental import pallas as pl
from jax.experimental.pallas import tpu as pltpu
from jax.sharding import PartitionSpec as P

AXES = ("row", "col")
BS = 128
ROWS = 6
BLOCKS = 12
SHARD = BLOCKS * BS
UNROLL = 4
MAX_PAIRS = 96 + 2 * UNROLL


def device_id(x, y, z, c):
    return ((x * 2 + y // 2) * 2 + c) * 16 + (y % 2) * 8 + z


def table(move, keep=lambda x, y, z, c: True):
    pairs = []
    for x in range(4):
        for y in range(4):
            for z in range(8):
                for c in range(2):
                    if keep(x, y, z, c):
                        tx, ty, tz, tc = move(x, y, z, c)
                        pairs.append((device_id(x, y, z, c), device_id(tx % 4, ty % 4, tz % 8, tc)))
    return pairs


def near(x, y, z, c):
    return x // 2 == y % 2


IN_PAIR = table(lambda x, y, z, c: (x ^ 1, y, z, c))
CROSS = table(lambda x, y, z, c: (3 - x, y, z, c))
CROSS_NEAR = table(lambda x, y, z, c: (3 - x, y, z, c), near)
Y_FAR_NEAR = table(lambda x, y, z, c: (x, y + 2, z, c), near)
Y_UP = table(lambda x, y, z, c: (x, y + 1, z, c))
Y_DOWN = table(lambda x, y, z, c: (x, y - 1, z, c))
Y_LO = table(lambda x, y, z, c: (x, y ^ 1, z, c))
CORE = table(lambda x, y, z, c: (x, y, z, 1 - c))
Z_GROUPS = [[g * 8 + z for z in range(8)] for g in range(2)]


def send(value, pairs):
    return lax.ppermute(value, AXES, pairs)


def kernel(ids, slots, left, *refs):
    right = refs[:8]
    out = refs[8]
    lbuf, rbuf, acc, pl_l, pl_r, pl_o, lsem, rsem = refs[9:]
    first_k = slots[8]

    for q in range(8):
        pltpu.make_async_copy(left.at[q, pl.ds(0, SHARD), :], lbuf.at[pl.ds(q * SHARD, SHARD), :], lsem).start()
    for n in range(8):
        at = pl.multiple_of(slots[n] * SHARD, SHARD)
        pltpu.make_async_copy(right[n].at[pl.ds(0, SHARD), :], rbuf.at[pl.ds(at, SHARD), :], rsem).start()

    zero_block = 8 * BLOCKS
    rbuf[pl.ds(zero_block * BS, BS), :] = jnp.zeros((BS, BS), jnp.float32)
    acc[...] = jnp.zeros_like(acc)

    def list_output(o, n):
        i = o // 2
        j = ids[16 * 16 + o]
        for q in range(8):
            for t in range(2):
                lb = q * BLOCKS + i * 2 + t
                k = ids[q * 16 + i * 2 + t] - (first_k + q * ROWS)
                at = (8 + q) * 16 + k * 2
                m1 = (ids[at + 1] == j).astype(jnp.int32)
                m0 = (ids[at] == j).astype(jnp.int32)
                pl_l[n] = lb
                pl_r[n] = q * BLOCKS + k * 2 + m1
                pl_o[n // 2] = o
                n = n + m0 + m1
        pl_l[n] = 0
        pl_r[n] = zero_block
        return n + n % 2

    n = lax.fori_loop(0, BLOCKS, list_output, 0)
    pairs = n // 2
    for u in range(UNROLL):
        pl_o[pairs + u] = BLOCKS
        for h in range(2):
            pl_l[n + 2 * u + h] = 0
            pl_r[n + 2 * u + h] = zero_block

    for q in range(8):
        pltpu.make_async_copy(left.at[q, pl.ds(0, SHARD), :], lbuf.at[pl.ds(q * SHARD, SHARD), :], lsem).wait()
        pltpu.make_async_copy(right[q].at[pl.ds(0, SHARD), :], rbuf.at[pl.ds(q * SHARD, SHARD), :], rsem).wait()

    def split(a):
        hi = a.astype(jnp.bfloat16)
        return hi, (a - hi.astype(jnp.float32)).astype(jnp.bfloat16)

    def block(buf, b):
        return buf[pl.ds(pl.multiple_of(b * BS, BS), BS), :]

    def step(s, carry):
        results = []
        for u in range(UNROLL):
            e = s * UNROLL + u
            a = jnp.concatenate([block(lbuf, pl_l[2 * e]), block(lbuf, pl_l[2 * e + 1])], axis=1)
            b = jnp.concatenate([block(rbuf, pl_r[2 * e]), block(rbuf, pl_r[2 * e + 1])], axis=0)
            a = jnp.concatenate(split(a), axis=0)
            b = jnp.concatenate(split(b), axis=1)
            r = jnp.dot(a, b, preferred_element_type=jnp.float32)
            results.append(r[:BS, :BS] + (r[:BS, BS:] + r[BS:, :BS]) + r[BS:, BS:])
        for u in range(UNROLL):
            o = pl_o[s * UNROLL + u]
            acc[o] = acc[o] + results[u]
        return carry

    lax.fori_loop(0, (pairs + UNROLL - 1) // UNROLL, step, 0)
    out[...] = acc[:BLOCKS]


def contract(ids, slots, left, right):
    return pl.pallas_call(
        kernel,
        out_shape=jax.ShapeDtypeStruct((BLOCKS, BS, BS), jnp.float32),
        in_specs=[pl.BlockSpec(memory_space=pltpu.SMEM)] * 2 + [pl.BlockSpec(memory_space=pl.ANY)] * 9,
        out_specs=pl.BlockSpec(memory_space=pltpu.VMEM),
        scratch_shapes=[
            pltpu.VMEM((8 * SHARD, BS), jnp.float32),
            pltpu.VMEM((8 * SHARD + BS, BS), jnp.float32),
            pltpu.VMEM((BLOCKS + 1, BS, BS), jnp.float32),
            pltpu.SMEM((2 * MAX_PAIRS + 2,), jnp.int32),
            pltpu.SMEM((2 * MAX_PAIRS + 2,), jnp.int32),
            pltpu.SMEM((MAX_PAIRS + 1,), jnp.int32),
            pltpu.SemaphoreType.DMA,
            pltpu.SemaphoreType.DMA,
        ],
        compiler_params=pltpu.CompilerParams(vmem_limit_bytes=40 * 2 ** 20),
        cost_estimate=pl.CostEstimate(flops=3 * 10 ** 9, bytes_accessed=13 * 10 ** 6, transcendentals=0),
    )(ids, slots, left, *right)


def body(iterate, kept_cols):
    row, col = lax.axis_index("row"), lax.axis_index("col")
    x, y_hi, core = row // 4, (row // 2) % 2, row % 2
    y_lo, z = col // 8, col % 8
    is_near = (x // 2) == y_lo
    first_x = jnp.where(is_near, x, 3 - x)

    ids8 = jnp.pad(kept_cols.reshape(1, BLOCKS).astype(jnp.float32), ((0, 7), (0, BS - BLOCKS)))
    own = jnp.concatenate([iterate.reshape(SHARD, BS), ids8], axis=0)

    left = lax.all_gather(own, "col", axis=0, tiled=False, axis_index_groups=Z_GROUPS)
    partner_ids = send(ids8, Y_LO)

    half = SHARD // 2
    in_pair, cross = send(own, IN_PAIR), send(own, CROSS)
    far = send(own, Y_FAR_NEAR)
    far_cross = send(far, CROSS_NEAR)
    nb1 = jnp.where(is_near, cross, own)
    up1, down1 = send(nb1, Y_UP), send(nb1, Y_DOWN)
    diag = jnp.concatenate([send(in_pair[:half], CROSS), send(cross[half:], IN_PAIR)], axis=0)
    far1 = jnp.where(is_near, far, far_cross)
    far2 = send(far1, IN_PAIR)
    nb2 = jnp.where(is_near, diag, in_pair)
    up2, down2 = send(nb2, Y_UP), send(nb2, Y_DOWN)
    here1 = jnp.where(is_near, own, cross)
    here2 = jnp.where(is_near, in_pair, diag)

    def both_cores(parts):
        return parts + [send(v, CORE) for v in parts]

    def slots_of(x_bits, y_his):
        local = [xb % 2 * 4 + yh * 2 for xb, yh in zip(x_bits, y_his)]
        slots = [s + core for s in local] + [s + 1 - core for s in local]
        return jnp.stack(slots + [y_lo * 48]).astype(jnp.int32)

    def ids_of(parts, slots, out_ids):
        rows = jnp.stack([v[SHARD, :16] for v in parts])
        rows = jnp.zeros((8, 16), jnp.float32).at[slots[:8]].set(rows, unique_indices=True)
        rows = jnp.concatenate([left[:, SHARD, :16], rows, out_ids[:1, :16]], axis=0)
        return rows.astype(jnp.int32).reshape(-1)

    y = y_hi * 2 + y_lo
    below, above = (y - 1) % 4 // 2, (y + 1) % 4 // 2
    parts = both_cores([up1, down1, up2, down2])
    slots = slots_of([first_x, first_x, first_x + 1, first_x + 1], [below, above, below, above])
    partial = contract(ids_of(parts, slots, partner_ids), slots, left, parts)
    received = send(partial, Y_LO)

    parts = both_cores([here1, here2, far1, far2])
    slots = slots_of([first_x, first_x + 1, first_x, first_x + 1], [y_hi, y_hi, 1 - y_hi, 1 - y_hi])
    mine = contract(ids_of(parts, slots, ids8), slots, left, parts)

    square = (mine + received).reshape(iterate.shape)
    update = 1.5 * iterate - 0.5 * square
    return (square, update)


def solution(mesh):
    in_specs = (P("row", "col", None, None), P("row", "col"))
    out_specs = (P("row", "col", None, None), P("row", "col", None, None))
    return jax.shard_map(body, mesh=mesh, in_specs=in_specs, out_specs=out_specs, check_vma=False)
```

```python
import functools

import jax
import jax.numpy as jnp
from jax import lax
from jax.experimental import pallas as pl
from jax.experimental.pallas import tpu as pltpu
from jax.sharding import PartitionSpec as P

AXES = ("row", "col")
BS = 128
ROWS = 6
BLOCKS = 12
HALF = BLOCKS // 2 * BS
IDS = 8
PACKED = 2 * HALF + IDS
PIECE = HALF + IDS
UNROLL = 4


def device_id(x, y, z, c):
    return ((x * 2 + y // 2) * 2 + c) * 16 + (y % 2) * 8 + z


def table(move, keep=lambda x, y, z, c: True):
    pairs = []
    for x in range(4):
        for y in range(4):
            for z in range(8):
                for c in range(2):
                    if keep(x, y, z, c):
                        tx, ty, tz, tc = move(x, y, z, c)
                        pairs.append((device_id(x, y, z, c), device_id(tx % 4, ty % 4, tz % 8, tc)))
    return pairs


def near(x, y, z, c):
    return x // 2 == y % 2


IN_PAIR = table(lambda x, y, z, c: (x ^ 1, y, z, c))
CROSS = table(lambda x, y, z, c: (3 - x, y, z, c))
CROSS_NEAR = table(lambda x, y, z, c: (3 - x, y, z, c), near)
Y_FAR_NEAR = table(lambda x, y, z, c: (x, y + 2, z, c), near)
Y_UP = table(lambda x, y, z, c: (x, y + 1, z, c))
Y_DOWN = table(lambda x, y, z, c: (x, y - 1, z, c))
Y_LO = table(lambda x, y, z, c: (x, y ^ 1, z, c))
Z_SPLIT = table(lambda x, y, z, c: (x, y, z + 1 - 2 * c, c))
X_SPLIT = table(lambda x, y, z, c: (x ^ 1 if c else 3 - x, y, z, c))
CORE = table(lambda x, y, z, c: (x, y, z, 1 - c))
Z_UP = table(lambda x, y, z, c: (x, y, z + 1, c))
Z_DOWN = table(lambda x, y, z, c: (x, y, z - 1, c))


def send(value, pairs):
    return lax.ppermute(value, AXES, pairs)


def place():
    row, col = lax.axis_index("row"), lax.axis_index("col")
    return row // 4, (row // 2) % 2, row % 2, col // 8, col % 8


DISTANCES = (0, -1, 1, -2, 2, -3, 3)


def kernel(own_columns, last, started, *refs):
    distances = (() if last == "only" else DISTANCES) + (() if last == "without" else (4,))
    n_left = len(distances)
    lefts, refs = refs[:n_left], refs[n_left:]
    n_right = 9 if own_columns else 8
    rights, out_ids, refs = refs[:n_right], refs[n_right], refs[n_right + 1:]
    if started:
        start, refs = refs[0], refs[1:]
    out, lbuf, rbuf, acc, ids_l, ids_r, ids_o, list_l, list_r, list_o, sem, isem = refs
    zero_row = (1 if last == "only" else 8) * PACKED

    x, y_hi, core, y_lo, z = place()
    near_x = (x // 2) == y_lo
    flip = lax.rem(jnp.where(near_x, x, 3 - x), 2) * 4
    if own_columns:
        y_his = (y_hi, 1 - y_hi)
    else:
        y = y_hi * 2 + y_lo
        y_his = (lax.rem(y + 3, 4) // 2, lax.rem(y + 1, 4) // 2)

    def right_slot(n):
        other, chunk, which = n // 4, (n // 2) % 2, n % 2
        return chunk * 4 + y_his[which] * 2 + (1 - core if other else core)

    def right_copies(n, s):
        at = pl.multiple_of(s * PACKED, 8)
        id_copy = pltpu.make_async_copy(rights[n].at[pl.ds(HALF, IDS), :], ids_r.at[s], isem)
        if own_columns and n == 7:
            return (
                id_copy,
                pltpu.make_async_copy(rights[7].at[:, :], rbuf.at[pl.ds(at, PIECE), :], sem),
                pltpu.make_async_copy(rights[8].at[:, :], rbuf.at[pl.ds(at + PIECE, HALF), :], sem),
            )
        return id_copy, pltpu.make_async_copy(rights[n].at[:, :], rbuf.at[pl.ds(at, PACKED), :], sem)

    blocks_l = [lax.rem(z + distance + 8, 8) for distance in distances]
    slots_l = [block ^ flip for block in blocks_l]
    copies = [pltpu.make_async_copy(out_ids.at[:, :], ids_o, isem)]
    for n, distance in enumerate(distances):
        copies.append(pltpu.make_async_copy(lefts[n].at[pl.ds(HALF, IDS), :], ids_l.at[n], isem))
        at = n * PACKED
        copies.append(pltpu.make_async_copy(lefts[n].at[:, :], lbuf.at[pl.ds(at, PACKED), :], sem))
    if last != "only":
        for n in range(8):
            copies.extend(right_copies(n, right_slot(n)))
    for copy in copies:
        copy.start()
    if last == "only":
        for n in range(8):

            @pl.when(right_slot(n) == slots_l[0])
            def _(n=n):
                for copy in right_copies(n, 0):
                    copy.start()

        copies.extend(right_copies(0, 0))
        slots_r = [0]
    else:
        slots_r = slots_l

    rbuf[pl.ds(zero_row, BS), :] = jnp.zeros((BS, BS), jnp.float32)
    if started:
        acc[:BLOCKS] = start[...]
        acc[BLOCKS] = jnp.zeros((BS, BS), jnp.float32)
    else:
        acc[...] = jnp.zeros_like(acc)
    id_bytes = [copy for copy in copies if copy.dst_sem is isem]
    data_bytes = [copy for copy in copies if copy.dst_sem is sem]
    for copy in id_bytes:
        copy.wait()

    def list_output(o, n):
        i = o // 2
        skip = jnp.where(i >= 3, IDS, 0)
        j = ids_o[0, o]
        for m, block in enumerate(blocks_l):
            first_k = (y_lo * 8 + block) * ROWS
            for t in range(2):
                k = ids_l[m, 0, i * 2 + t].astype(jnp.int32) - first_k
                m1 = (ids_r[slots_r[m], 0, 2 * k + 1] == j).astype(jnp.int32)
                m0 = (ids_r[slots_r[m], 0, 2 * k] == j).astype(jnp.int32)
                list_l[n] = m * PACKED + t * BS + i * 2 * BS + skip
                list_r[n] = slots_r[m] * PACKED + (2 * k + m1) * BS + jnp.where(k >= 3, IDS, 0)
                list_o[n // 2] = o
                n = n + m0 + m1
        list_l[n] = 0
        list_r[n] = zero_row
        return n + n % 2

    n = lax.fori_loop(0, BLOCKS, list_output, 0)
    pairs = n // 2
    for u in range(UNROLL):
        list_o[pairs + u] = BLOCKS
        for e in range(2):
            list_l[n + 2 * u + e] = 0
            list_r[n + 2 * u + e] = zero_row
    for copy in data_bytes:
        copy.wait()

    def split(a):
        hi = a.astype(jnp.bfloat16)
        return hi, (a - hi.astype(jnp.float32)).astype(jnp.bfloat16)

    def left_block(e):
        return lbuf[pl.ds(pl.multiple_of(list_l[e], 8), BS), :]

    def right_block(e):
        return rbuf[pl.ds(pl.multiple_of(list_r[e], 8), BS), :]

    def step(s, carry):
        results = []
        for u in range(UNROLL):
            e = 2 * (s * UNROLL + u)
            a_hi, a_lo = split(jnp.concatenate([left_block(e), left_block(e + 1)], axis=1))
            b_hi, b_lo = split(jnp.concatenate([right_block(e), right_block(e + 1)], axis=0))
            a = jnp.concatenate([a_hi, a_lo], axis=0)
            b = jnp.concatenate([b_hi, b_lo], axis=1)
            r = jnp.dot(a, b, preferred_element_type=jnp.float32)
            results.append(r[:BS, :BS] + (r[:BS, BS:] + r[BS:, :BS]) + r[BS:, BS:])
        for u in range(UNROLL):
            o = list_o[s * UNROLL + u]
            acc[o] = acc[o] + results[u]
        return carry

    lax.fori_loop(0, (pairs + UNROLL - 1) // UNROLL, step, 0)
    out[...] = acc[:BLOCKS]


def contract(own_columns, last, lefts, rights, out_ids, start=None):
    n = {"with": 8, "without": 7, "only": 1}[last]
    longest = 12 * n * 2 + 2 * UNROLL + 2
    started = () if start is None else (start,)
    vmem = pl.BlockSpec(memory_space=pltpu.VMEM)
    return pl.pallas_call(
        functools.partial(kernel, own_columns, last, start is not None),
        out_shape=jax.ShapeDtypeStruct((BLOCKS, BS, BS), jnp.float32),
        in_specs=[pl.BlockSpec(memory_space=pl.ANY)] * (len(lefts) + len(rights) + 1) + [vmem] * len(started),
        out_specs=vmem,
        scratch_shapes=[
            pltpu.VMEM((n * PACKED, BS), jnp.float32),
            pltpu.VMEM(((1 if n == 1 else 8) * PACKED + BS, BS), jnp.float32),
            pltpu.VMEM((BLOCKS + 1, BS, BS), jnp.float32),
            pltpu.SMEM((n, IDS, BS), jnp.float32),
            pltpu.SMEM((1 if n == 1 else 8, IDS, BS), jnp.float32),
            pltpu.SMEM((IDS, BS), jnp.float32),
            pltpu.SMEM((longest,), jnp.int32),
            pltpu.SMEM((longest,), jnp.int32),
            pltpu.SMEM((longest // 2 + 1,), jnp.int32),
            pltpu.SemaphoreType.DMA,
            pltpu.SemaphoreType.DMA,
        ],
        compiler_params=pltpu.CompilerParams(vmem_limit_bytes=(8 if n == 1 else 30) * 2 ** 20),
        cost_estimate=pl.CostEstimate(flops=10 ** 6, bytes_accessed=10 ** 6, transcendentals=0),
    )(*lefts, *rights, out_ids, *started)


STRIPS = 4


def combine_kernel(mine, received, iterate, square, update, s_buf, u_buf, sems):
    copies = []
    for n in range(STRIPS):
        part = pl.ds(n * BLOCKS // STRIPS, BLOCKS // STRIPS)
        total = mine[part] + received[part]
        s_buf[part] = total
        u_buf[part] = 1.5 * iterate[part] - 0.5 * total
        for m, (buf, ref) in enumerate(((s_buf, square), (u_buf, update))):
            copies.append(pltpu.make_async_copy(buf.at[part], ref.at[part], sems.at[n, m]))
            copies[-1].start()
    for copy in copies:
        copy.wait()


def combine(mine, received, iterate):
    shape = jax.ShapeDtypeStruct((BLOCKS, BS, BS), jnp.float32)
    return pl.pallas_call(
        combine_kernel,
        out_shape=(shape, shape),
        in_specs=[pl.BlockSpec(memory_space=pltpu.VMEM)] * 3,
        out_specs=(pl.BlockSpec(memory_space=pl.ANY),) * 2,
        scratch_shapes=[
            pltpu.VMEM((BLOCKS, BS, BS), jnp.float32),
            pltpu.VMEM((BLOCKS, BS, BS), jnp.float32),
            pltpu.SemaphoreType.DMA((STRIPS, 2)),
        ],
        compiler_params=pltpu.CompilerParams(vmem_limit_bytes=8 * 2 ** 20),
    )(mine, received, iterate)


def body(iterate, kept_cols):
    x, y_hi, core, y_lo, z = place()
    is_near = (x // 2) == y_lo

    blocks = iterate.reshape(2 * HALF, BS)
    ids = jnp.pad(kept_cols.reshape(1, BLOCKS).astype(jnp.float32), ((0, IDS - 1), (0, BS - BLOCKS)))
    own = jnp.concatenate([blocks[:HALF], ids, blocks[HALF:]], axis=0)

    partner_ids = send(ids, Y_LO)
    up, down = own, own
    lefts = [own]
    for _ in range(3):
        up, down = send(up, Z_UP), send(down, Z_DOWN)
        lefts += [up, down]
    ends = [send(jnp.where(core == 0, up, down), Z_SPLIT)]

    mine, partner_ids = lax.optimization_barrier((own, partner_ids))
    in_pair, cross = send(mine, IN_PAIR), send(mine, CROSS)
    far = send(mine, Y_FAR_NEAR)
    next1 = jnp.where(is_near, cross, own)
    up1, down1 = send(next1, Y_UP), send(next1, Y_DOWN)
    in_pair, far = lax.optimization_barrier((in_pair, far))
    diagonal = send(jnp.where(core == 0, in_pair, cross), X_SPLIT)
    next2 = jnp.where(is_near, diagonal, in_pair)
    far, next2 = lax.optimization_barrier((far, next2))
    far_cross = send(far, CROSS_NEAR)
    up2, down2 = send(next2, Y_UP), send(next2, Y_DOWN)
    far1 = jnp.where(is_near, far, far_cross)
    far2 = send(far1, IN_PAIR)
    here1 = jnp.where(is_near, own, cross)
    here2 = jnp.where(is_near, in_pair, diagonal)

    swapped1 = [send(v, CORE) for v in (up1, down1)]
    up2, down2, far1, *lefts = lax.optimization_barrier((up2, down2, far1, *lefts))
    rights = [up1, down1, up2, down2] + swapped1 + [send(v, CORE) for v in (up2, down2)]
    partial = contract(False, "without", lefts, rights, partner_ids)
    here1, here2, far1, _ = lax.optimization_barrier((here1, here2, far1, up2))
    others = [send(v, CORE) for v in (here1, far1, here2)]
    partial, *others = lax.optimization_barrier((partial, *others))
    partial = contract(False, "only", ends, rights, partner_ids, partial)
    received = send(partial, Y_LO)

    far2, _ = lax.optimization_barrier((far2, partial))
    others += [send(far2[:PIECE], CORE), send(far2[PIECE:], CORE)]
    mine = contract(True, "with", lefts + ends, [here1, far1, here2, far2] + others, ids)

    square, update = combine(mine, received, iterate.reshape(BLOCKS, BS, BS))
    return (square.reshape(iterate.shape), update.reshape(iterate.shape))


def solution(mesh):
    in_specs = (P("row", "col", None, None), P("row", "col"))
    out_specs = (P("row", "col", None, None), P("row", "col", None, None))
    return jax.shard_map(body, mesh=mesh, in_specs=in_specs, out_specs=out_specs, check_vma=False)
```

```python
import functools

import jax
import jax.numpy as jnp
from jax import lax
from jax.experimental import pallas as pl
from jax.experimental.pallas import tpu as pltpu
from jax.sharding import PartitionSpec as P

AXES = ("row", "col")
BS = 128
ROWS = 6
BLOCKS = 12
HALF = BLOCKS // 2 * BS
IDS = 8
PACKED = 2 * HALF + IDS
PIECE = HALF + IDS
UNROLL = 8


def device_id(x, y, z, c):
    return ((x * 2 + y // 2) * 2 + c) * 16 + (y % 2) * 8 + z


def table(move, keep=lambda x, y, z, c: True):
    pairs = []
    for x in range(4):
        for y in range(4):
            for z in range(8):
                for c in range(2):
                    if keep(x, y, z, c):
                        tx, ty, tz, tc = move(x, y, z, c)
                        pairs.append((device_id(x, y, z, c), device_id(tx % 4, ty % 4, tz % 8, tc)))
    return pairs


def near(x, y, z, c):
    return x // 2 == y % 2


IN_PAIR = table(lambda x, y, z, c: (x ^ 1, y, z, c))
CROSS = table(lambda x, y, z, c: (3 - x, y, z, c))
CROSS_NEAR = table(lambda x, y, z, c: (3 - x, y, z, c), near)
Y_FAR_NEAR = table(lambda x, y, z, c: (x, y + 2, z, c), near)
Y_UP = table(lambda x, y, z, c: (x, y + 1, z, c))
Y_DOWN = table(lambda x, y, z, c: (x, y - 1, z, c))
Y_LO = table(lambda x, y, z, c: (x, y ^ 1, z, c))
Z_SPLIT = table(lambda x, y, z, c: (x, y, z + 1 - 2 * c, c))
X_SPLIT = table(lambda x, y, z, c: (x ^ 1 if c else 3 - x, y, z, c))
CORE = table(lambda x, y, z, c: (x, y, z, 1 - c))
Z_UP = table(lambda x, y, z, c: (x, y, z + 1, c))
Z_DOWN = table(lambda x, y, z, c: (x, y, z - 1, c))


def send(value, pairs):
    return lax.ppermute(value, AXES, pairs)


def place():
    row, col = lax.axis_index("row"), lax.axis_index("col")
    return row // 4, (row // 2) % 2, row % 2, col // 8, col % 8


DISTANCES = (0, -1, 1, -2, 2, -3, 3)


def kernel(own_columns, last, started, *refs):
    distances = (() if last == "only" else DISTANCES) + (() if last == "without" else (4,))
    n_left = len(distances)
    lefts, refs = refs[:n_left], refs[n_left:]
    n_right = 9 if own_columns else 8
    rights, out_ids, refs = refs[:n_right], refs[n_right], refs[n_right + 1:]
    if started:
        start, refs = refs[0], refs[1:]
    out, lbuf, rbuf, acc, ids_l, ids_r, ids_o, list_l, list_r, list_o, sem, isem = refs
    zero_row = (1 if last == "only" else 8) * PACKED

    x, y_hi, core, y_lo, z = place()
    near_x = (x // 2) == y_lo
    flip = lax.rem(jnp.where(near_x, x, 3 - x), 2) * 4
    if own_columns:
        y_his = (y_hi, 1 - y_hi)
    else:
        y = y_hi * 2 + y_lo
        y_his = (lax.rem(y + 3, 4) // 2, lax.rem(y + 1, 4) // 2)

    def right_slot(n):
        other, chunk, which = n // 4, (n // 2) % 2, n % 2
        return chunk * 4 + y_his[which] * 2 + (1 - core if other else core)

    def right_copies(n, s):
        at = pl.multiple_of(s * PACKED, 8)
        id_copy = pltpu.make_async_copy(rights[n].at[pl.ds(HALF, IDS), :], ids_r.at[s], isem)
        if own_columns and n == 7:
            return (
                id_copy,
                pltpu.make_async_copy(rights[7].at[:, :], rbuf.at[pl.ds(at, PIECE), :], sem),
                pltpu.make_async_copy(rights[8].at[:, :], rbuf.at[pl.ds(at + PIECE, HALF), :], sem),
            )
        return id_copy, pltpu.make_async_copy(rights[n].at[:, :], rbuf.at[pl.ds(at, PACKED), :], sem)

    blocks_l = [lax.rem(z + distance + 8, 8) for distance in distances]
    slots_l = [block ^ flip for block in blocks_l]
    copies = [pltpu.make_async_copy(out_ids.at[:, :], ids_o, isem)]
    for n, distance in enumerate(distances):
        copies.append(pltpu.make_async_copy(lefts[n].at[pl.ds(HALF, IDS), :], ids_l.at[n], isem))
        at = n * PACKED
        copies.append(pltpu.make_async_copy(lefts[n].at[:, :], lbuf.at[pl.ds(at, PACKED), :], sem))
    if last != "only":
        for n in range(8):
            copies.extend(right_copies(n, right_slot(n)))
    for copy in copies:
        copy.start()
    if last == "only":
        for n in range(8):

            @pl.when(right_slot(n) == slots_l[0])
            def _(n=n):
                for copy in right_copies(n, 0):
                    copy.start()

        copies.extend(right_copies(0, 0))
        slots_r = [0]
    else:
        slots_r = slots_l

    rbuf[pl.ds(zero_row, BS), :] = jnp.zeros((BS, BS), jnp.float32)
    if started:
        acc[:BLOCKS] = start[...]
        acc[BLOCKS] = jnp.zeros((BS, BS), jnp.float32)
    else:
        acc[...] = jnp.zeros_like(acc)
    id_bytes = [copy for copy in copies if copy.dst_sem is isem]
    data_bytes = [copy for copy in copies if copy.dst_sem is sem]
    for copy in id_bytes:
        copy.wait()

    def list_output(o, n):
        i = o // 2
        skip = jnp.where(i >= 3, IDS, 0)
        j = ids_o[0, o]
        for m, block in enumerate(blocks_l):
            first_k = (y_lo * 8 + block) * ROWS
            for t in range(2):
                k = ids_l[m, 0, i * 2 + t].astype(jnp.int32) - first_k
                m1 = (ids_r[slots_r[m], 0, 2 * k + 1] == j).astype(jnp.int32)
                m0 = (ids_r[slots_r[m], 0, 2 * k] == j).astype(jnp.int32)
                list_l[n] = m * PACKED + t * BS + i * 2 * BS + skip
                list_r[n] = slots_r[m] * PACKED + (2 * k + m1) * BS + jnp.where(k >= 3, IDS, 0)
                list_o[n // 2] = o
                n = n + m0 + m1
        list_l[n] = 0
        list_r[n] = zero_row
        return n + n % 2

    n = lax.fori_loop(0, BLOCKS, list_output, 0)
    pairs = n // 2
    for u in range(UNROLL):
        list_o[pairs + u] = BLOCKS
        for e in range(2):
            list_l[n + 2 * u + e] = 0
            list_r[n + 2 * u + e] = zero_row
    for copy in data_bytes:
        copy.wait()

    def split(a):
        hi = a.astype(jnp.bfloat16)
        return hi, (a - hi.astype(jnp.float32)).astype(jnp.bfloat16)

    def left_block(e):
        return lbuf[pl.ds(pl.multiple_of(list_l[e], 8), BS), :]

    def right_block(e):
        return rbuf[pl.ds(pl.multiple_of(list_r[e], 8), BS), :]

    def step(s, carry):
        results = []
        for u in range(UNROLL):
            e = 2 * (s * UNROLL + u)
            a_hi, a_lo = split(jnp.concatenate([left_block(e), left_block(e + 1)], axis=1))
            b_hi, b_lo = split(jnp.concatenate([right_block(e), right_block(e + 1)], axis=0))
            a = jnp.concatenate([a_hi, a_lo], axis=0)
            b = jnp.concatenate([b_hi, b_lo], axis=1)
            r = jnp.dot(a, b, preferred_element_type=jnp.float32)
            results.append(r[:BS, :BS] + (r[:BS, BS:] + r[BS:, :BS]) + r[BS:, BS:])
        for u in range(UNROLL):
            o = list_o[s * UNROLL + u]
            acc[o] = acc[o] + results[u]
        return carry

    lax.fori_loop(0, (pairs + UNROLL - 1) // UNROLL, step, 0)
    out[...] = acc[:BLOCKS]


def contract(own_columns, last, lefts, rights, out_ids, start=None):
    n = {"with": 8, "without": 7, "only": 1}[last]
    longest = 12 * n * 2 + 2 * UNROLL + 2
    started = () if start is None else (start,)
    vmem = pl.BlockSpec(memory_space=pltpu.VMEM)
    return pl.pallas_call(
        functools.partial(kernel, own_columns, last, start is not None),
        out_shape=jax.ShapeDtypeStruct((BLOCKS, BS, BS), jnp.float32),
        in_specs=[pl.BlockSpec(memory_space=pl.ANY)] * (len(lefts) + len(rights) + 1) + [vmem] * len(started),
        out_specs=vmem,
        scratch_shapes=[
            pltpu.VMEM((n * PACKED, BS), jnp.float32),
            pltpu.VMEM(((1 if n == 1 else 8) * PACKED + BS, BS), jnp.float32),
            pltpu.VMEM((BLOCKS + 1, BS, BS), jnp.float32),
            pltpu.SMEM((n, IDS, BS), jnp.float32),
            pltpu.SMEM((1 if n == 1 else 8, IDS, BS), jnp.float32),
            pltpu.SMEM((IDS, BS), jnp.float32),
            pltpu.SMEM((longest,), jnp.int32),
            pltpu.SMEM((longest,), jnp.int32),
            pltpu.SMEM((longest // 2 + 1,), jnp.int32),
            pltpu.SemaphoreType.DMA,
            pltpu.SemaphoreType.DMA,
        ],
        compiler_params=pltpu.CompilerParams(vmem_limit_bytes=(8 if n == 1 else 30) * 2 ** 20),
        cost_estimate=pl.CostEstimate(flops=10 ** 6, bytes_accessed=10 ** 6, transcendentals=0),
    )(*lefts, *rights, out_ids, *started)


STRIPS = 4


def combine_kernel(mine, received, iterate, square, update, s_buf, u_buf, sems):
    copies = []
    for n in range(STRIPS):
        part = pl.ds(n * BLOCKS // STRIPS, BLOCKS // STRIPS)
        total = mine[part] + received[part]
        s_buf[part] = total
        u_buf[part] = 1.5 * iterate[part] - 0.5 * total
        for m, (buf, ref) in enumerate(((s_buf, square), (u_buf, update))):
            copies.append(pltpu.make_async_copy(buf.at[part], ref.at[part], sems.at[n, m]))
            copies[-1].start()
    for copy in copies:
        copy.wait()


def combine(mine, received, iterate):
    shape = jax.ShapeDtypeStruct((BLOCKS, BS, BS), jnp.float32)
    return pl.pallas_call(
        combine_kernel,
        out_shape=(shape, shape),
        in_specs=[pl.BlockSpec(memory_space=pltpu.VMEM)] * 3,
        out_specs=(pl.BlockSpec(memory_space=pl.ANY),) * 2,
        scratch_shapes=[
            pltpu.VMEM((BLOCKS, BS, BS), jnp.float32),
            pltpu.VMEM((BLOCKS, BS, BS), jnp.float32),
            pltpu.SemaphoreType.DMA((STRIPS, 2)),
        ],
        compiler_params=pltpu.CompilerParams(vmem_limit_bytes=8 * 2 ** 20),
    )(mine, received, iterate)


def body(iterate, kept_cols):
    x, y_hi, core, y_lo, z = place()
    is_near = (x // 2) == y_lo

    blocks = iterate.reshape(2 * HALF, BS)
    ids = jnp.pad(kept_cols.reshape(1, BLOCKS).astype(jnp.float32), ((0, IDS - 1), (0, BS - BLOCKS)))
    own = jnp.concatenate([blocks[:HALF], ids, blocks[HALF:]], axis=0)

    partner_ids = send(ids, Y_LO)
    up, down = own, own
    lefts = [own]
    for _ in range(3):
        up, down = send(up, Z_UP), send(down, Z_DOWN)
        lefts += [up, down]
    ends = [send(jnp.where(core == 0, up, down), Z_SPLIT)]

    mine, partner_ids = lax.optimization_barrier((own, partner_ids))
    in_pair, cross = send(mine, IN_PAIR), send(mine, CROSS)
    far = send(mine, Y_FAR_NEAR)
    next1 = jnp.where(is_near, cross, own)
    up1, down1 = send(next1, Y_UP), send(next1, Y_DOWN)
    in_pair, far = lax.optimization_barrier((in_pair, far))
    diagonal = send(jnp.where(core == 0, in_pair, cross), X_SPLIT)
    next2 = jnp.where(is_near, diagonal, in_pair)
    far, next2 = lax.optimization_barrier((far, next2))
    far_cross = send(far, CROSS_NEAR)
    up2, down2 = send(next2, Y_UP), send(next2, Y_DOWN)
    far1 = jnp.where(is_near, far, far_cross)
    far2 = send(far1, IN_PAIR)
    here1 = jnp.where(is_near, own, cross)
    here2 = jnp.where(is_near, in_pair, diagonal)

    swapped1 = [send(v, CORE) for v in (up1, down1)]
    up2, down2, far1, swapped1, lefts = lax.optimization_barrier((up2, down2, far1, swapped1, lefts))
    rights = [up1, down1, up2, down2] + swapped1 + [send(v, CORE) for v in (up2, down2)]
    partial = contract(False, "without", lefts, rights, partner_ids)
    here1, _ = lax.optimization_barrier((here1, up2))
    other_here1 = send(here1, CORE)
    here2, far1, _ = lax.optimization_barrier((here2, far1, partial))
    others = [other_here1, send(far1, CORE), send(here2, CORE)]
    partial, others[0] = lax.optimization_barrier((partial, other_here1))
    partial = contract(False, "only", ends, rights, partner_ids, partial)
    received = send(partial, Y_LO)

    far2, _ = lax.optimization_barrier((far2, partial))
    others += [send(far2[:PIECE], CORE), send(far2[PIECE:], CORE)]
    mine = contract(True, "with", lefts + ends, [here1, far1, here2, far2] + others, ids)

    square, update = combine(mine, received, iterate.reshape(BLOCKS, BS, BS))
    return (square.reshape(iterate.shape), update.reshape(iterate.shape))


def solution(mesh):
    in_specs = (P("row", "col", None, None), P("row", "col"))
    out_specs = (P("row", "col", None, None), P("row", "col", None, None))
    return jax.shard_map(body, mesh=mesh, in_specs=in_specs, out_specs=out_specs, check_vma=False)
```

```python
import functools

import jax
import jax.numpy as jnp
from jax import lax
from jax.experimental import pallas as pl
from jax.experimental.pallas import tpu as pltpu
from jax.sharding import PartitionSpec as P

AXES = ("row", "col")
BS = 128
ROWS = 6
BLOCKS = 12
HALF = BLOCKS // 2 * BS
IDS = 8
PACKED = 2 * HALF + IDS
PIECE = HALF + IDS
UNROLL = 8


def device_id(x, y, z, c):
    return ((x * 2 + y // 2) * 2 + c) * 16 + (y % 2) * 8 + z


def table(move, keep=lambda x, y, z, c: True):
    pairs = []
    for x in range(4):
        for y in range(4):
            for z in range(8):
                for c in range(2):
                    if keep(x, y, z, c):
                        tx, ty, tz, tc = move(x, y, z, c)
                        pairs.append((device_id(x, y, z, c), device_id(tx % 4, ty % 4, tz % 8, tc)))
    return pairs


def near(x, y, z, c):
    return x // 2 == y % 2


IN_PAIR = table(lambda x, y, z, c: (x ^ 1, y, z, c))
CROSS = table(lambda x, y, z, c: (3 - x, y, z, c))
CROSS_NEAR = table(lambda x, y, z, c: (3 - x, y, z, c), near)
Y_FAR_NEAR = table(lambda x, y, z, c: (x, y + 2, z, c), near)
Y_UP = table(lambda x, y, z, c: (x, y + 1, z, c))
Y_DOWN = table(lambda x, y, z, c: (x, y - 1, z, c))
Y_LO = table(lambda x, y, z, c: (x, y ^ 1, z, c))
Z_SPLIT = table(lambda x, y, z, c: (x, y, z + 1 - 2 * c, c))
X_SPLIT = table(lambda x, y, z, c: (x ^ 1 if c else 3 - x, y, z, c))
CORE = table(lambda x, y, z, c: (x, y, z, 1 - c))
Z_UP = table(lambda x, y, z, c: (x, y, z + 1, c))
Z_DOWN = table(lambda x, y, z, c: (x, y, z - 1, c))


def send(value, pairs):
    return lax.ppermute(value, AXES, pairs)


def place():
    row, col = lax.axis_index("row"), lax.axis_index("col")
    return row // 4, (row // 2) % 2, row % 2, col // 8, col % 8


DISTANCES = (0, -1, 1, -2, 2, -3, 3)


def kernel(own_columns, last, started, *refs):
    distances = (() if last == "only" else DISTANCES) + (() if last == "without" else (4,))
    n_left = len(distances)
    lefts, refs = refs[:n_left], refs[n_left:]
    n_right = 9 if own_columns else 8
    rights, out_ids, refs = refs[:n_right], refs[n_right], refs[n_right + 1:]
    if started:
        start, refs = refs[0], refs[1:]
    out, lbuf, rbuf, acc, ids_l, ids_r, ids_o, list_l, list_r, list_o, sem, late_sem, isem = refs
    zero_row = (1 if last == "only" else 8) * PACKED

    x, y_hi, core, y_lo, z = place()
    near_x = (x // 2) == y_lo
    flip = lax.rem(jnp.where(near_x, x, 3 - x), 2) * 4
    if own_columns:
        y_his = (y_hi, 1 - y_hi)
    else:
        y = y_hi * 2 + y_lo
        y_his = (lax.rem(y + 3, 4) // 2, lax.rem(y + 1, 4) // 2)

    def right_slot(n):
        other, chunk, which = n // 4, (n // 2) % 2, n % 2
        return chunk * 4 + y_his[which] * 2 + (1 - core if other else core)

    def right_copies(n, s):
        at = pl.multiple_of(s * PACKED, 8)
        id_copy = pltpu.make_async_copy(rights[n].at[pl.ds(HALF, IDS), :], ids_r.at[s], isem)
        if own_columns and n == 7:
            return (
                id_copy,
                pltpu.make_async_copy(rights[7].at[:, :], rbuf.at[pl.ds(at, PIECE), :], sem),
                pltpu.make_async_copy(rights[8].at[:, :], rbuf.at[pl.ds(at + PIECE, HALF), :], sem),
            )
        return id_copy, pltpu.make_async_copy(rights[n].at[:, :], rbuf.at[pl.ds(at, PACKED), :], sem)

    blocks_l = [lax.rem(z + distance + 8, 8) for distance in distances]
    slots_l = [block ^ flip for block in blocks_l]
    copies = [pltpu.make_async_copy(out_ids.at[:, :], ids_o, isem)]
    late = []
    for n, distance in enumerate(distances):
        copies.append(pltpu.make_async_copy(lefts[n].at[pl.ds(HALF, IDS), :], ids_l.at[n], isem))
        at = n * PACKED
        copies.append(
            pltpu.make_async_copy(lefts[n].at[pl.ds(0, PIECE), :], lbuf.at[pl.ds(at, PIECE), :], sem)
        )
        late.append(
            pltpu.make_async_copy(lefts[n].at[pl.ds(PIECE, HALF), :], lbuf.at[pl.ds(at + PIECE, HALF), :], late_sem)
        )
    if last != "only":
        for n in range(8):
            copies.extend(right_copies(n, right_slot(n)))
    for copy in copies:
        copy.start()
    if last == "only":
        for n in range(8):

            @pl.when(right_slot(n) == slots_l[0])
            def _(n=n):
                for copy in right_copies(n, 0):
                    copy.start()

        copies.extend(right_copies(0, 0))
        slots_r = [0]
    else:
        slots_r = slots_l

    for copy in late:
        copy.start()

    rbuf[pl.ds(zero_row, BS), :] = jnp.zeros((BS, BS), jnp.float32)
    if started:
        acc[:BLOCKS] = start[...]
        acc[BLOCKS] = jnp.zeros((BS, BS), jnp.float32)
    else:
        acc[...] = jnp.zeros_like(acc)
    id_bytes = [copy for copy in copies if copy.dst_sem is isem]
    data_bytes = [copy for copy in copies if copy.dst_sem is sem]
    for copy in id_bytes:
        copy.wait()

    def list_output(o, n):
        i = o // 2
        skip = jnp.where(i >= 3, IDS, 0)
        j = ids_o[0, o]
        for m, block in enumerate(blocks_l):
            first_k = (y_lo * 8 + block) * ROWS
            for t in range(2):
                k = ids_l[m, 0, i * 2 + t].astype(jnp.int32) - first_k
                m1 = (ids_r[slots_r[m], 0, 2 * k + 1] == j).astype(jnp.int32)
                m0 = (ids_r[slots_r[m], 0, 2 * k] == j).astype(jnp.int32)
                list_l[n] = m * PACKED + t * BS + i * 2 * BS + skip
                list_r[n] = slots_r[m] * PACKED + (2 * k + m1) * BS + jnp.where(k >= 3, IDS, 0)
                list_o[n // 2] = o
                n = n + m0 + m1
        list_l[n] = 0
        list_r[n] = zero_row
        return n + n % 2

    half_n = lax.fori_loop(0, BLOCKS // 2, list_output, 0)
    n = lax.fori_loop(BLOCKS // 2, BLOCKS, list_output, half_n)
    pairs = n // 2
    for u in range(UNROLL):
        list_o[pairs + u] = BLOCKS
        for e in range(2):
            list_l[n + 2 * u + e] = 0
            list_r[n + 2 * u + e] = zero_row
    for copy in data_bytes:
        copy.wait()

    def split(a):
        hi = a.astype(jnp.bfloat16)
        return hi, (a - hi.astype(jnp.float32)).astype(jnp.bfloat16)

    def left_block(e):
        return lbuf[pl.ds(pl.multiple_of(list_l[e], 8), BS), :]

    def right_block(e):
        return rbuf[pl.ds(pl.multiple_of(list_r[e], 8), BS), :]

    def step(s, carry):
        results = []
        for u in range(UNROLL):
            e = 2 * (s * UNROLL + u)
            a_hi, a_lo = split(jnp.concatenate([left_block(e), left_block(e + 1)], axis=1))
            b_hi, b_lo = split(jnp.concatenate([right_block(e), right_block(e + 1)], axis=0))
            a = jnp.concatenate([a_hi, a_lo], axis=0)
            b = jnp.concatenate([b_hi, b_lo], axis=1)
            r = jnp.dot(a, b, preferred_element_type=jnp.float32)
            results.append(r[:BS, :BS] + (r[:BS, BS:] + r[BS:, :BS]) + r[BS:, BS:])
        for u in range(UNROLL):
            o = list_o[s * UNROLL + u]
            acc[o] = acc[o] + results[u]
        return carry

    early = half_n // (2 * UNROLL)
    lax.fori_loop(0, early, step, 0)
    for copy in late:
        copy.wait()
    lax.fori_loop(early, (pairs + UNROLL - 1) // UNROLL, step, 0)
    out[...] = acc[:BLOCKS]


def contract(own_columns, last, lefts, rights, out_ids, start=None):
    n = {"with": 8, "without": 7, "only": 1}[last]
    longest = 12 * n * 2 + 2 * UNROLL + 2
    started = () if start is None else (start,)
    vmem = pl.BlockSpec(memory_space=pltpu.VMEM)
    return pl.pallas_call(
        functools.partial(kernel, own_columns, last, start is not None),
        out_shape=jax.ShapeDtypeStruct((BLOCKS, BS, BS), jnp.float32),
        in_specs=[pl.BlockSpec(memory_space=pl.ANY)] * (len(lefts) + len(rights) + 1) + [vmem] * len(started),
        out_specs=vmem,
        scratch_shapes=[
            pltpu.VMEM((n * PACKED, BS), jnp.float32),
            pltpu.VMEM(((1 if n == 1 else 8) * PACKED + BS, BS), jnp.float32),
            pltpu.VMEM((BLOCKS + 1, BS, BS), jnp.float32),
            pltpu.SMEM((n, IDS, BS), jnp.float32),
            pltpu.SMEM((1 if n == 1 else 8, IDS, BS), jnp.float32),
            pltpu.SMEM((IDS, BS), jnp.float32),
            pltpu.SMEM((longest,), jnp.int32),
            pltpu.SMEM((longest,), jnp.int32),
            pltpu.SMEM((longest // 2 + 1,), jnp.int32),
            pltpu.SemaphoreType.DMA,
            pltpu.SemaphoreType.DMA,
            pltpu.SemaphoreType.DMA,
        ],
        compiler_params=pltpu.CompilerParams(vmem_limit_bytes=(8 if n == 1 else 30) * 2 ** 20),
        cost_estimate=pl.CostEstimate(flops=10 ** 6, bytes_accessed=10 ** 6, transcendentals=0),
    )(*lefts, *rights, out_ids, *started)


STRIPS = 4


def combine_kernel(mine, received, iterate, square, update, s_buf, u_buf, sems):
    copies = []
    for n in range(STRIPS):
        part = pl.ds(n * BLOCKS // STRIPS, BLOCKS // STRIPS)
        total = mine[part] + received[part]
        s_buf[part] = total
        u_buf[part] = 1.5 * iterate[part] - 0.5 * total
        for m, (buf, ref) in enumerate(((s_buf, square), (u_buf, update))):
            copies.append(pltpu.make_async_copy(buf.at[part], ref.at[part], sems.at[n, m]))
            copies[-1].start()
    for copy in copies:
        copy.wait()


def combine(mine, received, iterate):
    shape = jax.ShapeDtypeStruct((BLOCKS, BS, BS), jnp.float32)
    return pl.pallas_call(
        combine_kernel,
        out_shape=(shape, shape),
        in_specs=[pl.BlockSpec(memory_space=pltpu.VMEM)] * 3,
        out_specs=(pl.BlockSpec(memory_space=pl.ANY),) * 2,
        scratch_shapes=[
            pltpu.VMEM((BLOCKS, BS, BS), jnp.float32),
            pltpu.VMEM((BLOCKS, BS, BS), jnp.float32),
            pltpu.SemaphoreType.DMA((STRIPS, 2)),
        ],
        compiler_params=pltpu.CompilerParams(vmem_limit_bytes=8 * 2 ** 20),
    )(mine, received, iterate)


def body(iterate, kept_cols):
    x, y_hi, core, y_lo, z = place()
    is_near = (x // 2) == y_lo

    blocks = iterate.reshape(2 * HALF, BS)
    ids = jnp.pad(kept_cols.reshape(1, BLOCKS).astype(jnp.float32), ((0, IDS - 1), (0, BS - BLOCKS)))
    own = jnp.concatenate([blocks[:HALF], ids, blocks[HALF:]], axis=0)

    partner_ids = send(ids, Y_LO)
    up, down = own, own
    lefts = [own]
    for _ in range(3):
        up, down = send(up, Z_UP), send(down, Z_DOWN)
        lefts += [up, down]
    ends = [send(jnp.where(core == 0, up, down), Z_SPLIT)]

    mine, partner_ids = lax.optimization_barrier((own, partner_ids))
    in_pair, cross = send(mine, IN_PAIR), send(mine, CROSS)
    far = send(mine, Y_FAR_NEAR)
    next1 = jnp.where(is_near, cross, own)
    up1, down1 = send(next1, Y_UP), send(next1, Y_DOWN)
    in_pair, far = lax.optimization_barrier((in_pair, far))
    diagonal = send(jnp.where(core == 0, in_pair, cross), X_SPLIT)
    next2 = jnp.where(is_near, diagonal, in_pair)
    far, next2 = lax.optimization_barrier((far, next2))
    far_cross = send(far, CROSS_NEAR)
    up2, down2 = send(next2, Y_UP), send(next2, Y_DOWN)
    far1 = jnp.where(is_near, far, far_cross)
    far2 = send(far1, IN_PAIR)
    here1 = jnp.where(is_near, own, cross)
    here2 = jnp.where(is_near, in_pair, diagonal)

    swapped1 = [send(v, CORE) for v in (up1, down1)]
    up2, down2, far1, swapped1, lefts = lax.optimization_barrier((up2, down2, far1, swapped1, lefts))
    rights = [up1, down1, up2, down2] + swapped1 + [send(v, CORE) for v in (up2, down2)]
    partial = contract(False, "without", lefts, rights, partner_ids)
    here1, _ = lax.optimization_barrier((here1, up2))
    other_here1 = send(here1, CORE)
    here2, far1, _ = lax.optimization_barrier((here2, far1, partial))
    others = [other_here1, send(far1, CORE), send(here2, CORE)]
    partial, others[0] = lax.optimization_barrier((partial, other_here1))
    partial = contract(False, "only", ends, rights, partner_ids, partial)
    received = send(partial, Y_LO)

    far2, _ = lax.optimization_barrier((far2, partial))
    others += [send(far2[:PIECE], CORE), send(far2[PIECE:], CORE)]
    mine = contract(True, "with", lefts + ends, [here1, far1, here2, far2] + others, ids)

    square, update = combine(mine, received, iterate.reshape(BLOCKS, BS, BS))
    return (square.reshape(iterate.shape), update.reshape(iterate.shape))


def solution(mesh):
    in_specs = (P("row", "col", None, None), P("row", "col"))
    out_specs = (P("row", "col", None, None), P("row", "col", None, None))
    return jax.shard_map(body, mesh=mesh, in_specs=in_specs, out_specs=out_specs, check_vma=False)
```
